256 devices in a mesh: dp: 32 (over z, y), tensor: 8 (over x, core).
Axes of the slice: x: 4, y: 4, z: 8, core: 2. Of those that a mesh axis runs over, the one named last changes fastest.
Arguments:
- hidden: bfloat16 [1024, 48, 8192], P('dp'), may hold values from -6 to 6
- norm_gain: bfloat16 [8192], replicated, may hold values from 0.099609375 to 1.8984375
- kv_weight: bfloat16 [2048, 8192], P('tensor', 'dp')
- lengths: int32 [1024], P('dp'), may hold values from 1 to 48, as said below
- owner: int32 [1024], P('dp'), may hold values from 0 to 31, as said below
Outputs:
- kv_cache: bfloat16 [1024, 48, 2048], P(('dp', 'tensor'))
The draws below stay inside these ranges and needn't reach their ends.
Inputs may be any that keep to these rules, and one draw needn't show every extreme that they name: Within the 32 sequences of one dp index every owner appears exactly once. `lengths`: some sequence has length 1 and some has length 48.
All inputs are finite; a program needn't handle non-finite values.
Results may differ from the reference program's by a relative error of at most 0.0053.
Values may be sent and summed in bfloat16 or wider, within the bound.
No kernel may reach another device: no remote copies, remote signals or barrier semaphores. Data moves between devices by JAX's collectives and lax.ppermute only.
A program may use at most 128 MiB of HBM per device.

```python
import jax
import jax.numpy as jnp
from jax import lax

D = 8192
KVH = 8
HD = 128
SPO = 1
PMAX = 48
SEQ_DEV = 32
SEQS = 1024
KVROWS = 2048


def draw_kv_weight(key, part):
    key = jax.random.fold_in(key, 11)
    row_key, column_key, entry_key = jax.random.split(key, 3)
    row_scale = jnp.exp(jax.random.uniform(row_key, (2 * KVH * HD, 1), jnp.float32, jnp.log(0.3), jnp.log(3.0)))
    column_noise = jnp.exp(jax.random.uniform(column_key, (1, D), jnp.float32, 0.0, jnp.log(10.0)))
    ramp = jnp.arange(D, dtype=jnp.float32)[None, :] / D
    column_scale = column_noise * jnp.exp(ramp * jnp.log(3.0)) / 9.0
    entries = jax.random.normal(entry_key, (2 * KVH * HD, D), jnp.float32)
    return (entries * row_scale * column_scale / jnp.sqrt(jnp.float32(D))).astype(jnp.bfloat16)


def draw_lengths(key, part):
    key = jax.random.fold_in(key, 5)
    cap_key, fullest_key, length_key, which_key = jax.random.split(key, 4)
    holders = SEQS // SEQ_DEV
    lowest_cap = PMAX - PMAX // 4
    caps = jax.random.randint(cap_key, (holders, 1), lowest_cap, PMAX + 1)
    fullest = jax.random.randint(fullest_key, (), 0, holders)
    caps = jnp.where(jnp.arange(holders)[:, None] == fullest, PMAX, caps)
    floors = (caps + 1) // 2
    drawn = jax.random.randint(length_key, (holders, SEQ_DEV), floors, caps + 1)
    which = jax.random.randint(which_key, (), 0, SEQ_DEV)
    drawn = drawn.at[fullest, which].set(PMAX)
    drawn = drawn.at[fullest, (which + 1) % SEQ_DEV].set(1)
    return drawn.reshape(SEQS).astype(jnp.int32)


def shuffled_block(block_key):
    return jax.random.permutation(block_key, SEQ_DEV)


def draw_owner(key, part):
    key = jax.random.fold_in(key, 7)
    holders = SEQS // SEQ_DEV
    block_keys = jax.random.split(key, holders)
    shuffled = jax.vmap(shuffled_block)(block_keys)
    return (shuffled // SPO).reshape(SEQS).astype(jnp.int32)


def levels(key, extent, cuts, smallest, top_value):
    level = 1.0
    for axis_at, blocks in cuts:
        steps = jax.random.uniform(jax.random.fold_in(jax.random.fold_in(key, 6), axis_at), (blocks,), jnp.float32, smallest / len(cuts), top_value / len(cuts))
        level = level * jnp.repeat(jnp.exp(steps), extent[axis_at] // blocks).reshape((-1,) + (1,) * (len(extent) - 1 - axis_at))
    return level


def gaussian(own_key, extent, scale, bound, cuts=(), held_as=jnp.bfloat16):
    values = scale * jax.random.normal(own_key, extent, jnp.float32)
    if cuts:
        values = values * levels(own_key, extent, cuts, -0.22, 0.18)
    return jnp.clip(values, -bound, bound).astype(held_as)


def setup_inputs(seed: int = 0) -> dict:
    seeds = jax.random.split(jax.random.key(seed), 6)
    return {
        "hidden": gaussian(seeds[0], (SEQS, PMAX, D), 1.0, 6.0, ((0, 32),)),
        "norm_gain": jnp.clip(1.0 + 0.18 * jax.random.normal(seeds[1], (D,), jnp.float32), 0.099609375, 1.8984375).astype(jnp.bfloat16),
        "kv_weight": draw_kv_weight(jax.random.fold_in(seeds[5], 71), 0),
        "lengths": draw_lengths(jax.random.fold_in(seeds[5], 71), 0),
        "owner": draw_owner(jax.random.fold_in(seeds[5], 71), 0),
    }


EPSILON = 1e-05
WEIGHT_EPSILON = 1e-12
SATURATION = 2.0
ROPE_BASE = 500000.0

def saturate(weight, threshold):
    wide = weight.astype(jnp.float32)
    return jnp.clip(wide, -threshold[:, None], threshold[:, None]).astype(jnp.bfloat16)

def normalize(row_block, gain):
    wide = row_block.astype(jnp.float32)
    scale = lax.rsqrt(lax.optimization_barrier(jnp.mean(wide * wide, axis=-1, keepdims=True)) + EPSILON)
    return (wide * scale * gain.astype(jnp.float32)).astype(jnp.bfloat16)

def rotary(keys, positions):
    head_dim = keys.shape[-1]
    half_dim = head_dim // 2
    frequency = ROPE_BASE ** (-(2.0 * jnp.arange(half_dim, dtype=jnp.float32)) / head_dim)
    angles = positions.astype(jnp.float32)[:, None, None] * frequency[None, None, :]
    cosine = jnp.cos(angles)
    sine = jnp.sin(angles)
    first = keys[..., :half_dim]
    second = keys[..., half_dim:]
    return jnp.concatenate([first * cosine - second * sine, second * cosine + first * sine], axis=-1)

def finish(raw_kv, positions, is_valid, head_dim):
    row_count = raw_kv.shape[0]
    shaped = raw_kv.reshape(row_count, -1, 2, head_dim)
    keys = rotary(shaped[:, :, 0, :], positions)
    values = shaped[:, :, 1, :]
    joined = jnp.stack([keys, values], axis=2).reshape(row_count, -1)
    return jnp.where(is_valid[:, None], joined, jnp.float32(0.0)).astype(jnp.bfloat16)

def reference(hidden, norm_gain, kv_weight, lengths, owner):
    wide = kv_weight.astype(jnp.float32)
    threshold = SATURATION * jnp.sqrt(lax.optimization_barrier(jnp.sum(wide * wide, axis=1)) / D + WEIGHT_EPSILON)
    codes = saturate(kv_weight, threshold)
    holders = SEQS // SEQ_DEV
    blocks = hidden.reshape(holders, SEQ_DEV * PMAX, D)
    positions = jnp.tile(jnp.arange(PMAX, dtype=jnp.int32), SEQ_DEV)
    live = jnp.arange(PMAX, dtype=jnp.int32)[None, None, :] < lengths.reshape(holders, SEQ_DEV)[:, :, None]
    live = live.reshape(holders, SEQ_DEV * PMAX)

    def one_holder(inputs):
        block, is_valid = inputs
        normed = normalize(block, norm_gain)
        raw_kv = lax.dot_general(normed, codes, (((1,), (1,)), ((), ())), preferred_element_type=jnp.float32)
        return finish(raw_kv, positions, is_valid, HD)
    computed = lax.map(one_holder, (blocks, live)).reshape(SEQS, PMAX, KVROWS)
    owner_grid = owner.reshape(holders, SEQ_DEV)
    owner_hot = (owner_grid[:, :, None] == jnp.arange(holders, dtype=jnp.int32)[None, None, :]).astype(jnp.int32)
    owner_rank = lax.optimization_barrier(jnp.sum(owner_hot * (jnp.cumsum(owner_hot, axis=1) - 1), axis=2))
    target = owner_grid * SEQ_DEV + jnp.arange(holders, dtype=jnp.int32)[:, None] * SPO + owner_rank
    target = target.reshape(SEQS).astype(jnp.int32)
    cache = jnp.zeros((SEQS, PMAX, KVROWS), jnp.bfloat16)
    return cache.at[target].set(computed)
```

```python
import functools

import jax
import jax.numpy as jnp
from jax import lax
from jax.experimental import pallas as pl
from jax.experimental.pallas import tpu as pltpu
from jax.sharding import Mesh
from jax.sharding import PartitionSpec as P

HD = 128
EPSILON = 1e-05
WEIGHT_EPSILON = 1e-12
SATURATION = 2.0
ROPE_BASE = 500000.0
NZ, NY = 8, 4
PER_STEP = 8
VMEM_LIMIT = 40 * 1024 * 1024


def from_z(value, step):
    return lax.ppermute(value, "z", [((s + step) % NZ, s) for s in range(NZ)])


def from_y(value, step):
    return lax.ppermute(value, "y", [((s + step) % NY, s) for s in range(NY)])


def gather_y_then_z(own):
    up, down, far = from_y(own, 1), from_y(own, -1), from_y(own, 2)
    pair, rest = jnp.concatenate([own, up], axis=0), jnp.concatenate([down, far], axis=0)
    dys, others = [0, 1], [-1, 2]
    pieces = [(pair, [(0, dy) for dy in dys]), (rest, [(0, dy) for dy in others])]
    pair_up = pair_down = pair
    rest_up = rest_down = rest
    for s in range(1, 4):
        pair_up, pair_down = from_z(pair_up, 1), from_z(pair_down, -1)
        rest_up, rest_down = from_z(rest_up, 1), from_z(rest_down, -1)
        pieces += [(pair_up, [(s, dy) for dy in dys]), (pair_down, [(-s, dy) for dy in dys])]
        pieces += [(rest_up, [(s, dy) for dy in others]), (rest_down, [(-s, dy) for dy in others])]
    pieces.append((from_z(pair_up, 1), [(4, dy) for dy in dys]))
    pieces.append((from_z(rest_down, -1), [(4, dy) for dy in others]))
    return pieces


def gather_z_then_y(own):
    up1, down1 = from_z(own, 1), from_z(own, -1)
    up2, down2 = from_z(own, 2), from_z(own, -2)
    near, near_dz = jnp.concatenate([own, up1, down1, up2], axis=0), [0, 1, -1, 2]
    near_up, near_down = from_y(near, 1), from_y(near, -1)
    up3, down3, up4 = from_z(up2, 1), from_z(down2, -1), from_z(up2, 2)
    late, late_dz = jnp.concatenate([down2, up3, down3, up4], axis=0), [-2, 3, -3, 4]
    late_up, late_down = from_y(late, 1), from_y(late, -1)
    pieces = []
    for array, dzs, dy in (
        (near, near_dz, 0),
        (late, late_dz, 0),
        (near_up, near_dz, 1),
        (near_down, near_dz, -1),
        (late_up, late_dz, 1),
        (late_down, late_dz, -1),
        (from_y(near_up, 1), near_dz, 2),
        (from_y(late_down, -1), late_dz, 2),
    ):
        pieces.append((array, [(dz, dy) for dz in dzs]))
    return pieces


def write_codes(meta, place_ref, gain_ref, piece_refs, out_ref):
    z, y = place_ref[0], place_ref[1]
    rows, width = out_ref.shape
    blocks = [(ref, n, dz, dy) for ref, offsets in zip(piece_refs, meta) for n, (dz, dy) in enumerate(offsets)]
    cols = piece_refs[0].shape[2]
    total = jnp.zeros((rows, HD), jnp.float32)
    for ref, n, _, _ in blocks:
        for c in range(0, cols, HD):
            wide = ref[n, :, c : c + HD].astype(jnp.float32)
            total += wide * wide
    squares = jnp.sum(total, axis=1, keepdims=True)
    threshold = SATURATION * jnp.sqrt(squares / width + WEIGHT_EPSILON)
    high = jnp.broadcast_to(threshold.astype(jnp.bfloat16), (rows, cols))
    for ref, n, dz, dy in blocks:
        at = (((z + dz + NZ) % NZ) * NY + (y + dy + NY) % NY) * cols
        at = pl.multiple_of(at, cols)
        code = jnp.minimum(jnp.maximum(ref[n], -high), high)
        out_ref[:, pl.ds(at, cols)] = code * gain_ref[:, pl.ds(at, cols)]


def project_kernel(meta, place_ref, slot_ref, length_ref, hidden_ref, cosine_ref, sine_ref, gain_ref, *refs):
    piece_refs, refs = refs[: len(meta)], refs[len(meta) :]
    outs, (codes_ref, result_ref) = refs[:NZ], refs[NZ:]
    count, cap, width = hidden_ref.shape
    step = pl.program_id(0)

    @pl.when(step == 0)
    def _():
        write_codes(meta, place_ref, gain_ref, piece_refs, codes_ref)

    raw = lax.dot_general(
        hidden_ref[...].reshape(count * cap, width),
        codes_ref[...],
        (((1,), (1,)), ((), ())),
        preferred_element_type=jnp.float32,
    )
    position = lax.broadcasted_iota(jnp.int32, (cap, HD), 0)
    for j in range(count):
        squares = jnp.zeros((cap, HD), jnp.float32)
        for c in range(0, width, HD):
            wide = hidden_ref[j, :, c : c + HD].astype(jnp.float32)
            squares += wide * wide
        mean = jnp.sum(squares, axis=1, keepdims=True) / width
        scale = jnp.broadcast_to(lax.rsqrt(mean + EPSILON), (cap, HD))
        sequence = step * count + j
        scale = jnp.where(position < length_ref[sequence], scale, 0.0)
        keys = raw[j * cap : (j + 1) * cap, :HD] * scale
        values = raw[j * cap : (j + 1) * cap, HD:] * scale
        keys = keys * cosine_ref[...] + pltpu.roll(keys, HD // 2, 1) * sine_ref[...]
        slot = slot_ref[sequence]
        result_ref[slot, :, :HD] = keys.astype(jnp.bfloat16)
        result_ref[slot, :, HD:] = values.astype(jnp.bfloat16)

    @pl.when(step == pl.num_programs(0) - 1)
    def _():
        for k, out in enumerate(outs):
            out[...] = result_ref[k * NY : (k + 1) * NY]


def project(place, slot, lengths, hidden, cosine, sine, pieces, gain):
    seqs, cap, width = hidden.shape
    rows = pieces[0][0].shape[1]
    smem = pl.BlockSpec(memory_space=pltpu.SMEM)
    whole = lambda shape: pl.BlockSpec(shape, lambda i: (0,) * len(shape))
    return pl.pallas_call(
        functools.partial(project_kernel, [m for _, m in pieces]),
        grid=(seqs // PER_STEP,),
        out_shape=[jax.ShapeDtypeStruct((NY, cap, rows), jnp.bfloat16)] * NZ,
        in_specs=[smem] * 3
        + [pl.BlockSpec((PER_STEP, cap, width), lambda i: (i, 0, 0))]
        + [whole(a.shape) for a in (cosine, sine, gain)]
        + [whole(a.shape) for a, _ in pieces],
        out_specs=[whole((NY, cap, rows))] * NZ,
        scratch_shapes=[pltpu.VMEM((rows, width), jnp.bfloat16), pltpu.VMEM((seqs, cap, rows), jnp.bfloat16)],
        compiler_params=pltpu.CompilerParams(vmem_limit_bytes=VMEM_LIMIT),
        cost_estimate=pl.CostEstimate(
            flops=2 * seqs * cap * width * rows, bytes_accessed=2 * seqs * cap * width, transcendentals=0
        ),
        name="project",
    )(place, slot, lengths, hidden, cosine, sine, gain, *[a for a, _ in pieces])


def arrange_kernel(place_ref, *refs):
    ins, out = refs[:-1], refs[-1]
    z = place_ref[0]
    for k, ref in enumerate(ins):
        source = (z + NZ - k) % NZ
        for j in range(NY):
            out[j, source] = ref[j]


def arrange(received, place):
    ny, cap, rows = received[0].shape
    vmem = pl.BlockSpec(memory_space=pltpu.VMEM)
    return pl.pallas_call(
        arrange_kernel,
        out_shape=jax.ShapeDtypeStruct((ny, NZ, cap, rows), jnp.bfloat16),
        in_specs=[pl.BlockSpec(memory_space=pltpu.SMEM)] + [vmem] * NZ,
        out_specs=vmem,
        compiler_params=pltpu.CompilerParams(vmem_limit_bytes=16 * 1024 * 1024),
        name="arrange",
    )(place, *received)


ORDER = (4, 3, 5, 2, 6, 1, 7, 0)


def run(gather, own, hidden, gain, place, slot, lengths, cosine, sine):
    outs = project(place, slot, lengths, hidden, cosine, sine, gather(own), gain)
    received = [None] * NZ
    for k in ORDER:
        received[k] = from_z(outs[k], -k) if k else outs[k]
    return arrange(received, place)


def shards(hidden, norm_gain, kv_weight, lengths, owner):
    _, cap, width = hidden.shape
    rows, cols = kv_weight.shape
    z, y = lax.axis_index("z"), lax.axis_index("y")
    place = jnp.stack([z, y]).astype(jnp.int32)
    own = kv_weight.reshape(1, rows, cols)

    slot = ((owner // NY - z + NZ) % NZ * NY + owner % NY).astype(jnp.int32)

    frequency = ROPE_BASE ** (-(2.0 * jnp.arange(HD // 2, dtype=jnp.float32)) / HD)
    angles = jnp.arange(cap, dtype=jnp.float32)[:, None] * frequency[None, :]
    cosine = jnp.concatenate([jnp.cos(angles)] * 2, axis=1)
    sine = jnp.concatenate([-jnp.sin(angles), jnp.sin(angles)], axis=1)

    grouped = lax.cond(
        lax.axis_index("c") == 0,
        functools.partial(run, gather_y_then_z),
        functools.partial(run, gather_z_then_y),
        own, hidden, norm_gain.reshape(1, width), place, slot, lengths, cosine, sine,
    )
    landed = lax.all_to_all(
        grouped.reshape(NY * NZ, cap, rows), ("y", "x", "c"), split_axis=0, concat_axis=0, tiled=True
    )
    landed = landed.reshape(NY, NZ, cap, rows)
    return jnp.transpose(landed, (0, 2, 1, 3)).reshape(NY, cap, NZ * rows)


def solution(mesh):
    split = Mesh(mesh.devices.reshape(NZ, NY, 4, 2), ("z", "y", "x", "c"))
    dp, tensor = ("z", "y"), ("x", "c")
    return jax.shard_map(
        shards,
        mesh=split,
        in_specs=(P(dp, None, None), P(), P(tensor, dp), P(dp), P(dp)),
        out_specs=P(("z", "y", "x", "c"), None, None),
        check_vma=False,
    )
```

```python
import functools

import jax
import jax.numpy as jnp
from jax import lax
from jax.experimental import pallas as pl
from jax.experimental.pallas import tpu as pltpu
from jax.sharding import Mesh
from jax.sharding import PartitionSpec as P

HD = 128
EPSILON = 1e-05
WEIGHT_EPSILON = 1e-12
SATURATION = 2.0
ROPE_BASE = 500000.0
NZ, NY = 8, 4
PER_STEP = 8
VMEM_LIMIT = 40 * 1024 * 1024


def from_z(value, step):
    return lax.ppermute(value, "z", [((s + step) % NZ, s) for s in range(NZ)])


def from_y(value, step):
    return lax.ppermute(value, "y", [((s + step) % NY, s) for s in range(NY)])


def gather_y_then_z(own):
    up, down, far = from_y(own, 1), from_y(own, -1), from_y(own, 2)
    pair, rest = jnp.concatenate([own, up], axis=0), jnp.concatenate([down, far], axis=0)
    dys, others = [0, 1], [-1, 2]
    pieces = [(pair, [(0, dy) for dy in dys]), (rest, [(0, dy) for dy in others])]
    pair_up = pair_down = pair
    rest_up = rest_down = rest
    for s in range(1, 4):
        pair_up, pair_down = from_z(pair_up, 1), from_z(pair_down, -1)
        rest_up, rest_down = from_z(rest_up, 1), from_z(rest_down, -1)
        pieces += [(pair_up, [(s, dy) for dy in dys]), (pair_down, [(-s, dy) for dy in dys])]
        pieces += [(rest_up, [(s, dy) for dy in others]), (rest_down, [(-s, dy) for dy in others])]
    pieces.append((from_z(pair_up, 1), [(4, dy) for dy in dys]))
    pieces.append((from_z(rest_down, -1), [(4, dy) for dy in others]))
    return pieces


def gather_z_then_y(own):
    up1, down1 = from_z(own, 1), from_z(own, -1)
    up2, down2 = from_z(own, 2), from_z(own, -2)
    near, near_dz = jnp.concatenate([own, up1, down1, up2], axis=0), [0, 1, -1, 2]
    near_up, near_down = from_y(near, 1), from_y(near, -1)
    up3, down3, up4 = from_z(up2, 1), from_z(down2, -1), from_z(up2, 2)
    late, late_dz = jnp.concatenate([down2, up3, down3, up4], axis=0), [-2, 3, -3, 4]
    late_up, late_down = from_y(late, 1), from_y(late, -1)
    pieces = []
    for array, dzs, dy in (
        (near, near_dz, 0),
        (late, late_dz, 0),
        (near_up, near_dz, 1),
        (near_down, near_dz, -1),
        (late_up, late_dz, 1),
        (late_down, late_dz, -1),
        (from_y(near_up, 1), near_dz, 2),
        (from_y(late_down, -1), late_dz, 2),
    ):
        pieces.append((array, [(dz, dy) for dz in dzs]))
    return pieces


def write_codes(meta, place_ref, gain_ref, piece_refs, out_ref):
    z, y = place_ref[0], place_ref[1]
    rows, width = out_ref.shape
    blocks = [(ref, n, dz, dy) for ref, offsets in zip(piece_refs, meta) for n, (dz, dy) in enumerate(offsets)]
    cols = piece_refs[0].shape[2]
    total = jnp.zeros((rows, HD), jnp.float32)
    for ref, n, _, _ in blocks:
        for c in range(0, cols, HD):
            wide = ref[n, :, c : c + HD].astype(jnp.float32)
            total += wide * wide
    squares = jnp.sum(total, axis=1, keepdims=True)
    threshold = SATURATION * jnp.sqrt(squares / width + WEIGHT_EPSILON)
    high = jnp.broadcast_to(threshold.astype(jnp.bfloat16), (rows, cols))
    for ref, n, dz, dy in blocks:
        at = (((z + dz + NZ) % NZ) * NY + (y + dy + NY) % NY) * cols
        at = pl.multiple_of(at, cols)
        code = jnp.minimum(jnp.maximum(ref[n], -high), high)
        out_ref[:, pl.ds(at, cols)] = code * gain_ref[:, pl.ds(at, cols)]


def project_kernel(meta, place_ref, slot_ref, length_ref, hidden_ref, cosine_ref, sine_ref, gain_ref, *refs):
    piece_refs, refs = refs[: len(meta)], refs[len(meta) :]
    result_ref, codes_ref = refs
    count, cap, width = hidden_ref.shape
    step = pl.program_id(0)

    @pl.when(step == 0)
    def _():
        write_codes(meta, place_ref, gain_ref, piece_refs, codes_ref)

    raw = lax.dot_general(
        hidden_ref[...].reshape(count * cap, width),
        codes_ref[...],
        (((1,), (1,)), ((), ())),
        preferred_element_type=jnp.float32,
    )
    position = lax.broadcasted_iota(jnp.int32, (cap, HD), 0)
    for j in range(count):
        squares = jnp.zeros((cap, HD), jnp.float32)
        for c in range(0, width, HD):
            wide = hidden_ref[j, :, c : c + HD].astype(jnp.float32)
            squares += wide * wide
        mean = jnp.sum(squares, axis=1, keepdims=True) / width
        scale = jnp.broadcast_to(lax.rsqrt(mean + EPSILON), (cap, HD))
        sequence = step * count + j
        scale = jnp.where(position < length_ref[sequence], scale, 0.0)
        keys = raw[j * cap : (j + 1) * cap, :HD] * scale
        values = raw[j * cap : (j + 1) * cap, HD:] * scale
        keys = keys * cosine_ref[...] + pltpu.roll(keys, HD // 2, 1) * sine_ref[...]
        slot = slot_ref[sequence]
        result_ref[slot, :, :HD] = keys.astype(jnp.bfloat16)
        result_ref[slot, :, HD:] = values.astype(jnp.bfloat16)


def project(place, slot, lengths, hidden, cosine, sine, pieces, gain):
    seqs, cap, width = hidden.shape
    rows = pieces[0][0].shape[1]
    smem = pl.BlockSpec(memory_space=pltpu.SMEM)
    whole = lambda shape: pl.BlockSpec(shape, lambda i: (0,) * len(shape))
    return pl.pallas_call(
        functools.partial(project_kernel, [m for _, m in pieces]),
        grid=(seqs // PER_STEP,),
        out_shape=jax.ShapeDtypeStruct((seqs, cap, rows), jnp.bfloat16),
        in_specs=[smem] * 3
        + [pl.BlockSpec((PER_STEP, cap, width), lambda i: (i, 0, 0))]
        + [whole(a.shape) for a in (cosine, sine, gain)]
        + [whole(a.shape) for a, _ in pieces],
        out_specs=whole((seqs, cap, rows)),
        scratch_shapes=[pltpu.VMEM((rows, width), jnp.bfloat16)],
        compiler_params=pltpu.CompilerParams(vmem_limit_bytes=VMEM_LIMIT),
        cost_estimate=pl.CostEstimate(
            flops=2 * seqs * cap * width * rows, bytes_accessed=2 * seqs * cap * width, transcendentals=0
        ),
        name="project",
    )(place, slot, lengths, hidden, cosine, sine, gain, *[a for a, _ in pieces])


def run(gather, own, hidden, gain, place, slot, lengths, cosine, sine):
    by_target = project(place, slot, lengths, hidden, cosine, sine, gather(own), gain.reshape(1, -1))
    return lax.all_to_all(by_target, ("z", "y"), split_axis=0, concat_axis=0, tiled=True)


def shards(hidden, norm_gain, kv_weight, lengths, owner):
    _, cap, width = hidden.shape
    rows, cols = kv_weight.shape
    z, y = lax.axis_index("z"), lax.axis_index("y")
    place = jnp.stack([z, y]).astype(jnp.int32)
    own = kv_weight.reshape(1, rows, cols)

    frequency = ROPE_BASE ** (-(2.0 * jnp.arange(HD // 2, dtype=jnp.float32)) / HD)
    angles = jnp.arange(cap, dtype=jnp.float32)[:, None] * frequency[None, :]
    cosine = jnp.concatenate([jnp.cos(angles)] * 2, axis=1)
    sine = jnp.concatenate([-jnp.sin(angles), jnp.sin(angles)], axis=1)

    grouped = lax.cond(
        lax.axis_index("c") == 0,
        functools.partial(run, gather_y_then_z),
        functools.partial(run, gather_z_then_y),
        own, hidden, norm_gain, place, owner, lengths, cosine, sine,
    )
    landed = lax.all_to_all(grouped, ("x", "c"), split_axis=0, concat_axis=0, tiled=True)
    landed = landed.reshape(-1, NY, cap, rows)
    return jnp.transpose(landed, (1, 2, 0, 3)).reshape(NY, cap, -1)


def solution(mesh):
    split = Mesh(mesh.devices.reshape(NZ, NY, 4, 2), ("z", "y", "x", "c"))
    dp, tensor = ("z", "y"), ("x", "c")
    return jax.shard_map(
        shards,
        mesh=split,
        in_specs=(P(dp, None, None), P(), P(tensor, dp), P(dp), P(dp)),
        out_specs=P(("z", "y", "x", "c"), None, None),
        check_vma=False,
    )
```

```python
import functools

import jax
import jax.numpy as jnp
from jax import lax
from jax.experimental import pallas as pl
from jax.experimental.pallas import tpu as pltpu
from jax.sharding import Mesh
from jax.sharding import PartitionSpec as P

HD = 128
EPSILON = 1e-05
WEIGHT_EPSILON = 1e-12
SATURATION = 2.0
ROPE_BASE = 500000.0
NZ, NY = 8, 4
PER_STEP = 8
VMEM_LIMIT = 40 * 1024 * 1024


def from_z(value, step):
    return lax.ppermute(value, "z", [((s + step) % NZ, s) for s in range(NZ)])


def from_y(value, step):
    return lax.ppermute(value, "y", [((s + step) % NY, s) for s in range(NY)])


def gather_y_then_z(own):
    up, down, far = from_y(own, 1), from_y(own, -1), from_y(own, 2)
    pair, rest = jnp.concatenate([own, up], axis=0), jnp.concatenate([down, far], axis=0)
    dys, others = [0, 1], [-1, 2]
    pieces = [(pair, [(0, dy) for dy in dys]), (rest, [(0, dy) for dy in others])]
    pair_up = pair_down = pair
    rest_up = rest_down = rest
    for s in range(1, 4):
        pair_up, pair_down = from_z(pair_up, 1), from_z(pair_down, -1)
        rest_up, rest_down = from_z(rest_up, 1), from_z(rest_down, -1)
        pieces += [(pair_up, [(s, dy) for dy in dys]), (pair_down, [(-s, dy) for dy in dys])]
        pieces += [(rest_up, [(s, dy) for dy in others]), (rest_down, [(-s, dy) for dy in others])]
    pieces.append((from_z(pair_up, 1), [(4, dy) for dy in dys]))
    pieces.append((from_z(rest_down, -1), [(4, dy) for dy in others]))
    return pieces


def gather_z_then_y(own):
    up1, down1 = from_z(own, 1), from_z(own, -1)
    up2, down2 = from_z(own, 2), from_z(own, -2)
    near, near_dz = jnp.concatenate([own, up1, down1, up2], axis=0), [0, 1, -1, 2]
    near_up, near_down = from_y(near, 1), from_y(near, -1)
    up3, down3, up4 = from_z(up2, 1), from_z(down2, -1), from_z(up2, 2)
    late, late_dz = jnp.concatenate([down2, up3, down3, up4], axis=0), [-2, 3, -3, 4]
    late_up, late_down = from_y(late, 1), from_y(late, -1)
    pieces = []
    for array, dzs, dy in (
        (near, near_dz, 0),
        (late, late_dz, 0),
        (near_up, near_dz, 1),
        (near_down, near_dz, -1),
        (late_up, late_dz, 1),
        (late_down, late_dz, -1),
        (from_y(near_up, 1), near_dz, 2),
        (from_y(late_down, -1), late_dz, 2),
    ):
        pieces.append((array, [(dz, dy) for dz in dzs]))
    return pieces


def write_codes(meta, place_ref, gain_ref, piece_refs, out_ref):
    z, y = place_ref[0], place_ref[1]
    rows, width = out_ref.shape
    blocks = [(ref, n, dz, dy) for ref, offsets in zip(piece_refs, meta) for n, (dz, dy) in enumerate(offsets)]
    cols = piece_refs[0].shape[2]
    total = jnp.zeros((rows, HD), jnp.float32)
    for ref, n, _, _ in blocks:
        for c in range(0, cols, HD):
            wide = ref[n, :, c : c + HD].astype(jnp.float32)
            total += wide * wide
    squares = jnp.sum(total, axis=1, keepdims=True)
    threshold = SATURATION * jnp.sqrt(squares / width + WEIGHT_EPSILON)
    high = jnp.broadcast_to(threshold.astype(jnp.bfloat16), (rows, cols))
    for ref, n, dz, dy in blocks:
        at = (((z + dz + NZ) % NZ) * NY + (y + dy + NY) % NY) * cols
        at = pl.multiple_of(at, cols)
        code = jnp.minimum(jnp.maximum(ref[n], -high), high)
        out_ref[:, pl.ds(at, cols)] = code * gain_ref[:, pl.ds(at, cols)]


def project_kernel(meta, place_ref, slot_ref, length_ref, hidden_ref, cosine_ref, sine_ref, gain_ref, *refs):
    piece_refs, refs = refs[: len(meta)], refs[len(meta) :]
    result_ref, codes_ref = refs
    count, cap, width = hidden_ref.shape
    step = pl.program_id(0)

    @pl.when(step == 0)
    def _():
        write_codes(meta, place_ref, gain_ref, piece_refs, codes_ref)

    raw = lax.dot_general(
        hidden_ref[...].reshape(count * cap, width),
        codes_ref[...],
        (((1,), (1,)), ((), ())),
        preferred_element_type=jnp.float32,
    )
    position = lax.broadcasted_iota(jnp.int32, (cap, HD), 0)
    for j in range(count):
        squares = jnp.zeros((cap, HD), jnp.float32)
        for c in range(0, width, HD):
            wide = hidden_ref[j, :, c : c + HD].astype(jnp.float32)
            squares += wide * wide
        mean = jnp.sum(squares, axis=1, keepdims=True) / width
        scale = jnp.broadcast_to(lax.rsqrt(mean + EPSILON), (cap, HD))
        sequence = step * count + j
        scale = jnp.where(position < length_ref[sequence], scale, 0.0)
        keys = raw[j * cap : (j + 1) * cap, :HD] * scale
        values = raw[j * cap : (j + 1) * cap, HD:] * scale
        keys = keys * cosine_ref[...] + pltpu.roll(keys, HD // 2, 1) * sine_ref[...]
        slot = slot_ref[sequence]
        result_ref[slot, :, :HD] = keys.astype(jnp.bfloat16)
        result_ref[slot, :, HD:] = values.astype(jnp.bfloat16)


def project(place, slot, lengths, hidden, cosine, sine, pieces, gain):
    seqs, cap, width = hidden.shape
    rows = pieces[0][0].shape[1]
    smem = pl.BlockSpec(memory_space=pltpu.SMEM)
    whole = lambda shape: pl.BlockSpec(shape, lambda i: (0,) * len(shape))
    return pl.pallas_call(
        functools.partial(project_kernel, [m for _, m in pieces]),
        grid=(seqs // PER_STEP,),
        out_shape=jax.ShapeDtypeStruct((seqs, cap, rows), jnp.bfloat16),
        in_specs=[smem] * 3
        + [pl.BlockSpec((PER_STEP, cap, width), lambda i: (i, 0, 0))]
        + [whole(a.shape) for a in (cosine, sine, gain)]
        + [whole(a.shape) for a, _ in pieces],
        out_specs=whole((seqs, cap, rows)),
        scratch_shapes=[pltpu.VMEM((rows, width), jnp.bfloat16)],
        compiler_params=pltpu.CompilerParams(vmem_limit_bytes=VMEM_LIMIT),
        cost_estimate=pl.CostEstimate(
            flops=2 * seqs * cap * width * rows, bytes_accessed=2 * seqs * cap * width, transcendentals=0
        ),
        name="project",
    )(place, slot, lengths, hidden, cosine, sine, gain, *[a for a, _ in pieces])


def run(gather, own, hidden, gain, place, slot, lengths, cosine, sine):
    by_target = project(place, slot, lengths, hidden, cosine, sine, gather(own), gain.reshape(1, -1))
    return lax.all_to_all(by_target, ("z", "y"), split_axis=0, concat_axis=0, tiled=True)


def side_by_side_kernel(heads_ref, out_ref, sems):
    heads, _, _, rows = heads_ref.shape
    copies = [
        pltpu.make_async_copy(heads_ref.at[t], out_ref.at[:, :, pl.ds(t * rows, rows)], sems.at[t]) for t in range(heads)
    ]
    for copy in copies:
        copy.start()
    for copy in copies:
        copy.wait()


def side_by_side(landed):
    heads, slots, cap, rows = landed.shape
    anywhere = pl.BlockSpec(memory_space=pl.ANY)
    return pl.pallas_call(
        side_by_side_kernel,
        out_shape=jax.ShapeDtypeStruct((slots, cap, heads * rows), landed.dtype),
        in_specs=[anywhere],
        out_specs=anywhere,
        scratch_shapes=[pltpu.SemaphoreType.DMA((heads,))],
        name="side_by_side",
    )(landed)


def shards(hidden, norm_gain, kv_weight, lengths, owner):
    _, cap, width = hidden.shape
    rows, cols = kv_weight.shape
    z, y = lax.axis_index("z"), lax.axis_index("y")
    place = jnp.stack([z, y]).astype(jnp.int32)
    own = kv_weight.reshape(1, rows, cols)

    frequency = ROPE_BASE ** (-(2.0 * jnp.arange(HD // 2, dtype=jnp.float32)) / HD)
    angles = jnp.arange(cap, dtype=jnp.float32)[:, None] * frequency[None, :]
    cosine = jnp.concatenate([jnp.cos(angles)] * 2, axis=1)
    sine = jnp.concatenate([-jnp.sin(angles), jnp.sin(angles)], axis=1)

    grouped = lax.cond(
        lax.axis_index("c") == 0,
        functools.partial(run, gather_y_then_z),
        functools.partial(run, gather_z_then_y),
        own, hidden, norm_gain, place, owner, lengths, cosine, sine,
    )
    landed = lax.all_to_all(grouped, ("x", "c"), split_axis=0, concat_axis=0, tiled=True)
    return side_by_side(landed.reshape(-1, NY, cap, rows))


def solution(mesh):
    split = Mesh(mesh.devices.reshape(NZ, NY, 4, 2), ("z", "y", "x", "c"))
    dp, tensor = ("z", "y"), ("x", "c")
    return jax.shard_map(
        shards,
        mesh=split,
        in_specs=(P(dp, None, None), P(), P(tensor, dp), P(dp), P(dp)),
        out_specs=P(("z", "y", "x", "c"), None, None),
        check_vma=False,
    )
```

```python
import functools

import jax
import jax.numpy as jnp
from jax import lax
from jax.experimental import pallas as pl
from jax.experimental.pallas import tpu as pltpu
from jax.sharding import Mesh
from jax.sharding import PartitionSpec as P

HD = 128
EPSILON = 1e-05
WEIGHT_EPSILON = 1e-12
SATURATION = 2.0
ROPE_BASE = 500000.0
NZ, NY = 8, 4
PER_STEP = 8
VMEM_LIMIT = 40 * 1024 * 1024


def from_z(value, step):
    return lax.ppermute(value, "z", [((s + step) % NZ, s) for s in range(NZ)])


def from_y(value, step):
    return lax.ppermute(value, "y", [((s + step) % NY, s) for s in range(NY)])


def gather_y_then_z(own):
    up, down, far = from_y(own, 1), from_y(own, -1), from_y(own, 2)
    pair, rest = jnp.concatenate([own, up], axis=0), jnp.concatenate([down, far], axis=0)
    dys, others = [0, 1], [-1, 2]
    pieces = [(pair, [(0, dy) for dy in dys]), (rest, [(0, dy) for dy in others])]
    pair_up = pair_down = pair
    rest_up = rest_down = rest
    for s in range(1, 4):
        pair_up, pair_down = from_z(pair_up, 1), from_z(pair_down, -1)
        rest_up, rest_down = from_z(rest_up, 1), from_z(rest_down, -1)
        pieces += [(pair_up, [(s, dy) for dy in dys]), (pair_down, [(-s, dy) for dy in dys])]
        pieces += [(rest_up, [(s, dy) for dy in others]), (rest_down, [(-s, dy) for dy in others])]
    pieces.append((from_z(pair_up, 1), [(4, dy) for dy in dys]))
    pieces.append((from_z(rest_down, -1), [(4, dy) for dy in others]))
    return pieces


def gather_z_then_y(own):
    up1, down1 = from_z(own, 1), from_z(own, -1)
    up2, down2 = from_z(own, 2), from_z(own, -2)
    near, near_dz = jnp.concatenate([own, up1, down1, up2], axis=0), [0, 1, -1, 2]
    near_up, near_down = from_y(near, 1), from_y(near, -1)
    up3, down3, up4 = from_z(up2, 1), from_z(down2, -1), from_z(up2, 2)
    late, late_dz = jnp.concatenate([down2, up3, down3, up4], axis=0), [-2, 3, -3, 4]
    late_up, late_down = from_y(late, 1), from_y(late, -1)
    pieces = []
    for array, dzs, dy in (
        (near, near_dz, 0),
        (late, late_dz, 0),
        (near_up, near_dz, 1),
        (near_down, near_dz, -1),
        (late_up, late_dz, 1),
        (late_down, late_dz, -1),
        (from_y(near_up, 1), near_dz, 2),
        (from_y(late_down, -1), late_dz, 2),
    ):
        pieces.append((array, [(dz, dy) for dz in dzs]))
    return pieces


def write_codes(meta, place_ref, gain_ref, piece_refs, out_ref):
    z, y = place_ref[0], place_ref[1]
    rows, width = out_ref.shape
    blocks = [(ref, n, dz, dy) for ref, offsets in zip(piece_refs, meta) for n, (dz, dy) in enumerate(offsets)]
    cols = piece_refs[0].shape[2]
    total = jnp.zeros((rows, HD), jnp.float32)
    for ref, n, _, _ in blocks:
        for c in range(0, cols, HD):
            wide = ref[n, :, c : c + HD].astype(jnp.float32)
            total += wide * wide
    squares = jnp.sum(total, axis=1, keepdims=True)
    threshold = SATURATION * jnp.sqrt(squares / width + WEIGHT_EPSILON)
    high = jnp.broadcast_to(threshold.astype(jnp.bfloat16), (rows, cols))
    for ref, n, dz, dy in blocks:
        at = (((z + dz + NZ) % NZ) * NY + (y + dy + NY) % NY) * cols
        at = pl.multiple_of(at, cols)
        code = jnp.minimum(jnp.maximum(ref[n], -high), high)
        out_ref[:, pl.ds(at, cols)] = code * gain_ref[:, pl.ds(at, cols)]


def project_kernel(meta, place_ref, slot_ref, length_ref, hidden_ref, cosine_ref, sine_ref, gain_ref, *refs):
    piece_refs, refs = refs[: len(meta)], refs[len(meta) :]
    result_ref, codes_ref = refs
    count, cap, width = hidden_ref.shape
    step = pl.program_id(0)

    @pl.when(step == 0)
    def _():
        write_codes(meta, place_ref, gain_ref, piece_refs, codes_ref)

    raw = lax.dot_general(
        hidden_ref[...].reshape(count * cap, width),
        codes_ref[...],
        (((1,), (1,)), ((), ())),
        preferred_element_type=jnp.float32,
    )
    position = lax.broadcasted_iota(jnp.int32, (cap, HD), 0)
    for j in range(count):
        squares = jnp.zeros((cap, HD), jnp.float32)
        for c in range(0, width, HD):
            wide = hidden_ref[j, :, c : c + HD].astype(jnp.float32)
            squares += wide * wide
        mean = jnp.sum(squares, axis=1, keepdims=True) / width
        scale = jnp.broadcast_to(lax.rsqrt(mean + EPSILON), (cap, HD))
        sequence = step * count + j
        scale = jnp.where(position < length_ref[sequence], scale, 0.0)
        keys = raw[j * cap : (j + 1) * cap, :HD] * scale
        values = raw[j * cap : (j + 1) * cap, HD:] * scale
        keys = keys * cosine_ref[...] + pltpu.roll(keys, HD // 2, 1) * sine_ref[...]
        slot = slot_ref[sequence]
        result_ref[slot, :, :HD] = keys.astype(jnp.bfloat16)
        result_ref[slot, :, HD:] = values.astype(jnp.bfloat16)


def project(place, slot, lengths, hidden, cosine, sine, pieces, gain):
    seqs, cap, width = hidden.shape
    rows = pieces[0][0].shape[1]
    smem = pl.BlockSpec(memory_space=pltpu.SMEM)
    whole = lambda shape: pl.BlockSpec(shape, lambda i: (0,) * len(shape))
    return pl.pallas_call(
        functools.partial(project_kernel, [m for _, m in pieces]),
        grid=(seqs // PER_STEP,),
        out_shape=jax.ShapeDtypeStruct((seqs, cap, rows), jnp.bfloat16),
        in_specs=[smem] * 3
        + [pl.BlockSpec((PER_STEP, cap, width), lambda i: (i, 0, 0))]
        + [whole(a.shape) for a in (cosine, sine, gain)]
        + [whole(a.shape) for a, _ in pieces],
        out_specs=whole((seqs, cap, rows)),
        scratch_shapes=[pltpu.VMEM((rows, width), jnp.bfloat16)],
        compiler_params=pltpu.CompilerParams(vmem_limit_bytes=VMEM_LIMIT),
        cost_estimate=pl.CostEstimate(
            flops=2 * seqs * cap * width * rows, bytes_accessed=2 * seqs * cap * width, transcendentals=0
        ),
        name="project",
    )(place, slot, lengths, hidden, cosine, sine, gain, *[a for a, _ in pieces])


def run(gather, own, hidden, gain, place, slot, lengths, cosine, sine):
    by_target = project(place, slot, lengths, hidden, cosine, sine, gather(own), gain.reshape(1, -1))
    return lax.all_to_all(by_target, ("z", "y"), split_axis=0, concat_axis=0, tiled=True)


def side_by_side_kernel(heads_ref, out_ref):
    heads, _, _, rows = heads_ref.shape
    for t in range(heads):
        out_ref[:, :, t * rows : (t + 1) * rows] = heads_ref[t]


def side_by_side(landed):
    heads, slots, cap, rows = landed.shape
    vmem = pl.BlockSpec(memory_space=pltpu.VMEM)
    return pl.pallas_call(
        side_by_side_kernel,
        out_shape=jax.ShapeDtypeStruct((slots, cap, heads * rows), landed.dtype),
        in_specs=[vmem],
        out_specs=vmem,
        compiler_params=pltpu.CompilerParams(vmem_limit_bytes=VMEM_LIMIT),
        name="side_by_side",
    )(landed)


def shards(hidden, norm_gain, kv_weight, lengths, owner):
    _, cap, width = hidden.shape
    rows, cols = kv_weight.shape
    z, y = lax.axis_index("z"), lax.axis_index("y")
    place = jnp.stack([z, y]).astype(jnp.int32)
    own = kv_weight.reshape(1, rows, cols)

    frequency = ROPE_BASE ** (-(2.0 * jnp.arange(HD // 2, dtype=jnp.float32)) / HD)
    angles = jnp.arange(cap, dtype=jnp.float32)[:, None] * frequency[None, :]
    cosine = jnp.concatenate([jnp.cos(angles)] * 2, axis=1)
    sine = jnp.concatenate([-jnp.sin(angles), jnp.sin(angles)], axis=1)

    grouped = lax.cond(
        lax.axis_index("c") == 0,
        functools.partial(run, gather_y_then_z),
        functools.partial(run, gather_z_then_y),
        own, hidden, norm_gain, place, owner, lengths, cosine, sine,
    )
    landed = lax.all_to_all(grouped, ("x", "c"), split_axis=0, concat_axis=0, tiled=True)
    return side_by_side(landed.reshape(-1, NY, cap, rows))


def solution(mesh):
    split = Mesh(mesh.devices.reshape(NZ, NY, 4, 2), ("z", "y", "x", "c"))
    dp, tensor = ("z", "y"), ("x", "c")
    return jax.shard_map(
        shards,
        mesh=split,
        in_specs=(P(dp, None, None), P(), P(tensor, dp), P(dp), P(dp)),
        out_specs=P(("z", "y", "x", "c"), None, None),
        check_vma=False,
    )
```

```python
import functools

import jax
import jax.numpy as jnp
from jax import lax
from jax.experimental import pallas as pl
from jax.experimental.pallas import tpu as pltpu
from jax.sharding import Mesh
from jax.sharding import PartitionSpec as P

HD = 128
EPSILON = 1e-05
WEIGHT_EPSILON = 1e-12
SATURATION = 2.0
ROPE_BASE = 500000.0
NZ, NY = 8, 4
PER_STEP = 8
VMEM_LIMIT = 40 * 1024 * 1024


def from_z(value, step):
    return lax.ppermute(value, "z", [((s + step) % NZ, s) for s in range(NZ)])


def from_y(value, step):
    return lax.ppermute(value, "y", [((s + step) % NY, s) for s in range(NY)])


def gather_y_then_z(own):
    up, down, far = from_y(own, 1), from_y(own, -1), from_y(own, 2)
    pair, rest = jnp.concatenate([own, up], axis=0), jnp.concatenate([down, far], axis=0)
    dys, others = [0, 1], [-1, 2]
    pieces = [(pair, [(0, dy) for dy in dys]), (rest, [(0, dy) for dy in others])]
    pair_up = pair_down = pair
    rest_up = rest_down = rest
    for s in range(1, 4):
        pair_up, pair_down = from_z(pair_up, 1), from_z(pair_down, -1)
        rest_up, rest_down = from_z(rest_up, 1), from_z(rest_down, -1)
        pieces += [(pair_up, [(s, dy) for dy in dys]), (pair_down, [(-s, dy) for dy in dys])]
        pieces += [(rest_up, [(s, dy) for dy in others]), (rest_down, [(-s, dy) for dy in others])]
    pieces.append((from_z(pair_up, 1), [(4, dy) for dy in dys]))
    pieces.append((from_z(rest_down, -1), [(4, dy) for dy in others]))
    return pieces


def gather_z_then_y(own):
    up1, down1 = from_z(own, 1), from_z(own, -1)
    up2, down2 = from_z(own, 2), from_z(own, -2)
    near, near_dz = jnp.concatenate([own, up1, down1, up2], axis=0), [0, 1, -1, 2]
    near_up, near_down = from_y(near, 1), from_y(near, -1)
    up3, down3, up4 = from_z(up2, 1), from_z(down2, -1), from_z(up2, 2)
    late, late_dz = jnp.concatenate([down2, up3, down3, up4], axis=0), [-2, 3, -3, 4]
    late_up, late_down = from_y(late, 1), from_y(late, -1)
    pieces = []
    for array, dzs, dy in (
        (near, near_dz, 0),
        (late, late_dz, 0),
        (near_up, near_dz, 1),
        (near_down, near_dz, -1),
        (late_up, late_dz, 1),
        (late_down, late_dz, -1),
        (from_y(near_up, 1), near_dz, 2),
        (from_y(late_down, -1), late_dz, 2),
    ):
        pieces.append((array, [(dz, dy) for dz in dzs]))
    return pieces


def write_codes(meta, place_ref, gain_ref, piece_refs, out_ref):
    z, y = place_ref[0], place_ref[1]
    rows, width = out_ref.shape
    blocks = [(ref, n, dz, dy) for ref, offsets in zip(piece_refs, meta) for n, (dz, dy) in enumerate(offsets)]
    cols = piece_refs[0].shape[2]
    total = jnp.zeros((rows, HD), jnp.float32)
    for ref, n, _, _ in blocks:
        for c in range(0, cols, HD):
            wide = ref[n, :, c : c + HD].astype(jnp.float32)
            total += wide * wide
    squares = jnp.sum(total, axis=1, keepdims=True)
    threshold = SATURATION * jnp.sqrt(squares / width + WEIGHT_EPSILON)
    high = jnp.broadcast_to(threshold.astype(jnp.bfloat16), (rows, cols))
    for ref, n, dz, dy in blocks:
        at = (((z + dz + NZ) % NZ) * NY + (y + dy + NY) % NY) * cols
        at = pl.multiple_of(at, cols)
        code = jnp.minimum(jnp.maximum(ref[n], -high), high)
        out_ref[:, pl.ds(at, cols)] = code * gain_ref[:, pl.ds(at, cols)]


def project_kernel(meta, place_ref, slot_ref, length_ref, hidden_ref, cosine_ref, sine_ref, gain_ref, *refs):
    piece_refs, refs = refs[: len(meta)], refs[len(meta) :]
    result_ref, codes_ref = refs
    count, cap, width = hidden_ref.shape
    step = pl.program_id(0)

    @pl.when(step == 0)
    def _():
        write_codes(meta, place_ref, gain_ref, piece_refs, codes_ref)

    raw = lax.dot_general(
        hidden_ref[...].reshape(count * cap, width),
        codes_ref[...],
        (((1,), (1,)), ((), ())),
        preferred_element_type=jnp.float32,
    )
    position = lax.broadcasted_iota(jnp.int32, (cap, HD), 0)
    for j in range(count):
        squares = jnp.zeros((cap, HD), jnp.float32)
        for c in range(0, width, HD):
            wide = hidden_ref[j, :, c : c + HD].astype(jnp.float32)
            squares += wide * wide
        mean = jnp.sum(squares, axis=1, keepdims=True) / width
        scale = jnp.broadcast_to(lax.rsqrt(mean + EPSILON), (cap, HD))
        sequence = step * count + j
        scale = jnp.where(position < length_ref[sequence], scale, 0.0)
        keys = raw[j * cap : (j + 1) * cap, :HD] * scale
        values = raw[j * cap : (j + 1) * cap, HD:] * scale
        keys = keys * cosine_ref[...] + pltpu.roll(keys, HD // 2, 1) * sine_ref[...]
        slot = slot_ref[sequence]
        result_ref[slot, :, :HD] = keys.astype(jnp.bfloat16)
        result_ref[slot, :, HD:] = values.astype(jnp.bfloat16)


def project(place, slot, lengths, hidden, cosine, sine, pieces, gain):
    seqs, cap, width = hidden.shape
    rows = pieces[0][0].shape[1]
    smem = pl.BlockSpec(memory_space=pltpu.SMEM)
    whole = lambda shape: pl.BlockSpec(shape, lambda i: (0,) * len(shape))
    return pl.pallas_call(
        functools.partial(project_kernel, [m for _, m in pieces]),
        grid=(seqs // PER_STEP,),
        out_shape=jax.ShapeDtypeStruct((seqs, cap, rows), jnp.bfloat16),
        in_specs=[smem] * 3
        + [pl.BlockSpec((PER_STEP, cap, width), lambda i: (i, 0, 0))]
        + [whole(a.shape) for a in (cosine, sine, gain)]
        + [whole(a.shape) for a, _ in pieces],
        out_specs=whole((seqs, cap, rows)),
        scratch_shapes=[pltpu.VMEM((rows, width), jnp.bfloat16)],
        compiler_params=pltpu.CompilerParams(vmem_limit_bytes=VMEM_LIMIT),
        cost_estimate=pl.CostEstimate(
            flops=2 * seqs * cap * width * rows, bytes_accessed=2 * seqs * cap * width, transcendentals=0
        ),
        name="project",
    )(place, slot, lengths, hidden, cosine, sine, gain, *[a for a, _ in pieces])


def run(gather, own, hidden, gain, place, slot, lengths, cosine, sine):
    by_target = project(place, slot, lengths, hidden, cosine, sine, gather(own), gain.reshape(1, -1))
    return lax.all_to_all(by_target, ("z", "y"), split_axis=0, concat_axis=0, tiled=True)


def side_by_side_kernel(heads_ref, out_ref):
    heads, _, _, rows = heads_ref.shape
    for t in range(heads):
        out_ref[:, :, t * rows : (t + 1) * rows] = heads_ref[t]


def side_by_side(landed):
    heads, slots, cap, rows = landed.shape
    vmem = pl.BlockSpec(memory_space=pltpu.VMEM)
    return pl.pallas_call(
        side_by_side_kernel,
        out_shape=jax.ShapeDtypeStruct((slots, cap, heads * rows), landed.dtype),
        in_specs=[vmem],
        out_specs=vmem,
        compiler_params=pltpu.CompilerParams(vmem_limit_bytes=VMEM_LIMIT),
        name="side_by_side",
    )(landed)


def shards(hidden, norm_gain, kv_weight, lengths, owner):
    _, cap, width = hidden.shape
    rows, cols = kv_weight.shape
    z, y = lax.axis_index("z"), lax.axis_index("y")
    place = jnp.stack([z, y]).astype(jnp.int32)
    own = kv_weight.reshape(1, rows, cols)

    frequency = ROPE_BASE ** (-(2.0 * jnp.arange(HD // 2, dtype=jnp.float32)) / HD)
    angles = jnp.arange(cap, dtype=jnp.float32)[:, None] * frequency[None, :]
    cosine = jnp.concatenate([jnp.cos(angles)] * 2, axis=1)
    sine = jnp.concatenate([-jnp.sin(angles), jnp.sin(angles)], axis=1)

    grouped = lax.cond(
        lax.axis_index("c") == 0,
        functools.partial(run, gather_z_then_y),
        functools.partial(run, gather_y_then_z),
        own, hidden, norm_gain, place, owner, lengths, cosine, sine,
    )
    landed = lax.all_to_all(grouped, ("x", "c"), split_axis=0, concat_axis=0, tiled=True)
    return side_by_side(landed.reshape(-1, NY, cap, rows))


def solution(mesh):
    split = Mesh(mesh.devices.reshape(NZ, NY, 4, 2), ("z", "y", "x", "c"))
    dp, tensor = ("z", "y"), ("x", "c")
    return jax.shard_map(
        shards,
        mesh=split,
        in_specs=(P(dp, None, None), P(), P(tensor, dp), P(dp), P(dp)),
        out_specs=P(("z", "y", "x", "c"), None, None),
        check_vma=False,
    )
```
